128 devices in a mesh: dp: 32 (over x, y, z_hi), fsdp: 4 (over z_lo, core).
Axes of the slice: x: 4, y: 4, z: 4 (z_hi: 2, z_lo: 2; z = z_hi * 2 + z_lo), core: 2. Of those that a mesh axis runs over, the one named last changes fastest.
Arguments:
- image_feat: bfloat16 [98304, 1152], P(('dp', 'fsdp')), may hold values from -6 to 6
- text_emb: bfloat16 [98304, 1152], P(('dp', 'fsdp')), may hold values from -0.1875 to 0.1875
- head: bfloat16 [1152, 1152], P('fsdp'), may hold values from -0.0048828125 to 0.0048828125
- partner: int32 [98304], P(('dp', 'fsdp')), may hold values from 0 to 767, as said below
- scale: float32 [1], replicated, may hold values from 5 to 15
- bias: float32 [1], replicated, may hold values from -4 to -1
Outputs:
- head_grad: float32 [1152, 1152], P('fsdp')
- text_grad: float32 [98304, 1152], P(('dp', 'fsdp'))
The draws below stay inside these ranges and needn't reach their ends.
Inputs may be any that keep to these rules, and one draw needn't show every extreme that they name: `partner`: within each block of 768 rows every value appears exactly once.
All inputs are finite; a program needn't handle non-finite values.
Results may differ from the reference program's by a relative error of at most 0.0051.
Values may be sent and summed in bfloat16 or wider, within the bound.
No kernel may reach another device: no remote copies, remote signals or barrier semaphores. Data moves between devices by JAX's collectives and lax.ppermute only.
A program may use at most 128 MiB of HBM per device.

```python
import jax
import jax.numpy as jnp
from jax import lax

D = 1152
F = 1152
ROWS_DEV = 768
STEPS = 4
PAIRS = 98304
N_DP = 32
N_FSDP = 4


def draw_partner(key, part):
    key = jax.random.fold_in(key, 5)
    keys = jax.random.split(key, PAIRS // ROWS_DEV)
    blocks = jax.vmap(lambda single: jax.random.permutation(single, ROWS_DEV))(keys)
    return blocks.reshape(PAIRS).astype(jnp.int32)


def shard_levels(own_key, extent, cuts, smallest, high):
    loudness, own = 1.0, jax.random.fold_in(own_key, 6)
    for axis_at, blocks in cuts:
        draws = jnp.exp(jax.random.uniform(jax.random.fold_in(own, axis_at), (blocks,), jnp.float32, smallest / len(cuts), high / len(cuts)))
        loudness = loudness * jnp.repeat(draws, extent[axis_at] // blocks).reshape([-1 if axis == axis_at else 1 for axis in range(len(extent))])
    return loudness


def noise(own_key, dims, scale, bound, shards=(), kind=jnp.bfloat16):
    level = shard_levels(own_key, dims, shards, -0.22, 0.18) if shards else 1.0
    array = jax.random.normal(own_key, dims, jnp.float32) * scale * level
    return jnp.minimum(jnp.maximum(array, -bound), bound).astype(kind)


def setup_inputs(seed: int = 0) -> dict:
    splits = jax.random.split(jax.random.key(seed), 7)
    image_feat = noise(splits[0], (PAIRS, F), 1.0, 6.0, ((0, 128),))
    text_emb = noise(splits[1], (PAIRS, D), 0.03, 0.1875, ((0, 128),))
    head = noise(splits[2], (F, D), (F * D) ** -0.5, 0.0048828125, ((0, 4),))
    partner = draw_partner(jax.random.fold_in(splits[6], 71), 0)
    scale = jnp.clip(jax.random.uniform(splits[4], (1,), jnp.float32, 5.0, 15.0), 5.0, 15.0)
    bias = jnp.clip(jax.random.uniform(splits[5], (1,), jnp.float32, -4.0, -1.0), -4.0, -1.0)
    return dict(image_feat=image_feat, text_emb=text_emb, head=head, partner=partner, scale=scale, bias=bias)


def unit_rows(vec):
    inv = lax.rsqrt(lax.optimization_barrier(jnp.sum(vec * vec, axis=-1, keepdims=True)) + 1e-06)
    return (vec * inv, inv)

def reference(image_feat, text_emb, head, partner, scale, bias):
    proj = jnp.dot(image_feat, head, preferred_element_type=jnp.float32)
    img_unit, rx = unit_rows(proj)
    img_b = img_unit.astype(jnp.bfloat16)
    txt_unit, ry = unit_rows(text_emb.astype(jnp.float32))
    txt_b = txt_unit.astype(jnp.bfloat16)
    temper = scale[0]
    offset = bias[0]
    shape4 = (N_DP, N_FSDP, ROWS_DEV, D)
    img4 = img_b.reshape(shape4).astype(jnp.float32)
    txt4 = txt_b.reshape(shape4)
    match = partner.reshape(N_DP, N_FSDP, ROWS_DEV)
    onehot = (match[..., None] == jnp.arange(ROWS_DEV, dtype=jnp.int32)[None, None, None, :]).astype(jnp.float32)
    d_img = jnp.zeros(shape4, jnp.float32)
    d_txt = jnp.zeros(shape4, jnp.float32)
    for step in range(STEPS):
        paired = jnp.roll(txt4, step, axis=0).astype(jnp.float32)
        logits = temper * jnp.einsum('pqad,pqcd->pqac', img4, paired) + offset
        if step == 0:
            target = onehot
        else:
            target = jnp.zeros_like(onehot)
        grad_b = (jax.nn.sigmoid(logits) - target).astype(jnp.bfloat16)
        grad_b = lax.optimization_barrier(grad_b).astype(jnp.float32)
        d_img = d_img + jnp.einsum('pqac,pqcd->pqad', grad_b, paired)
        d_txt = d_txt + jnp.roll(jnp.einsum('pqac,pqad->pqcd', grad_b, img4), -step, axis=0)
    d_img = temper * d_img.reshape(PAIRS, D)
    d_proj = rx * (d_img - img_unit * lax.optimization_barrier(jnp.sum(img_unit * d_img, axis=-1, keepdims=True)))
    d_proj = d_proj.astype(jnp.bfloat16)
    head_grad = jnp.dot(image_feat.T, d_proj, preferred_element_type=jnp.float32) / ROWS_DEV
    d_txt = temper * d_txt.reshape(PAIRS, D)
    text_grad = ry * (d_txt - txt_unit * lax.optimization_barrier(jnp.sum(txt_unit * d_txt, axis=-1, keepdims=True)))
    return (head_grad, text_grad)
```

```python
import jax
import jax.numpy as jnp
from jax import lax
from jax.sharding import Mesh, PartitionSpec as P

AXES = ("x", "y", "zh", "zl", "c")
SIZES = (4, 4, 2, 2, 2)
CONTRACT_ROWS = (((0,), (0,)), ((), ()))
CONTRACT_COLS = (((1,), (1,)), ((), ()))


def index_of(x, y, z, c):
    return ((x % 4 * 4 + y % 4) * 4 + z % 4) * 2 + c


def moved(value, target):
    pairs = [
        (index_of(x, y, z, c), index_of(*target(x, y, z, c)))
        for x in range(4)
        for y in range(4)
        for z in range(4)
        for c in range(2)
    ]
    return lax.ppermute(value, AXES, pairs)


def along_dp(value, by):
    pairs = [(d * 4 + j, (d + by) % 32 * 4 + j) for d in range(32) for j in range(4)]
    return lax.ppermute(value, AXES, pairs)


def unit_rows(vec):
    inv = lax.rsqrt(jnp.sum(vec * vec, axis=-1, keepdims=True) + 1e-06)
    return (vec * inv, inv)


def dot32(a, b, dims=(((1,), (0,)), ((), ()))):
    return lax.dot_general(a, b, dims, preferred_element_type=jnp.float32)


def gathered_head(head):
    x, zl, c = lax.axis_index("x"), lax.axis_index("zl"), lax.axis_index("c")
    half = head.shape[0] // 2
    mine = lax.dynamic_slice_in_dim(head, x % 2 * half, half, 0)
    got = moved(mine, lambda x, y, z, c: (x, y, z ^ 1, c))
    other = moved(got, lambda x, y, z, c: (x ^ 1, y, z, c))
    far = jnp.where(x % 2 == 0, jnp.concatenate([got, other]), jnp.concatenate([other, got]))
    both = jnp.where(zl == 0, jnp.stack([head, far]), jnp.stack([far, head]))
    swapped = moved(both, lambda x, y, z, c: (x, y, z, 1 - c))
    order = jnp.where(c == 0, jnp.stack([both, swapped], 1), jnp.stack([swapped, both], 1))
    return order.reshape(4 * head.shape[0], head.shape[1])


def reduced(part):
    x, zl, c = lax.axis_index("x"), lax.axis_index("zl"), lax.axis_index("c")
    width = part.shape[1]
    f32, b16 = jnp.float32, jnp.bfloat16
    part = part.reshape(2, 2, 288, width)

    def take(value, at, axis):
        return lax.dynamic_index_in_dim(value, at, axis, keepdims=False)

    got = moved(take(part, 1 - c, 1).astype(b16), lambda x, y, z, c: (x, y, z, 1 - c))
    part = take(part, c, 1) + got.astype(f32)
    part = part.reshape(2, 4, 72, width)
    sent = part.astype(b16)
    got = [
        moved(take(sent, (x + d) % 4, 1), lambda x, y, z, c, d=d: (x + d, y, z, c))
        for d in (2, 1, 3)
    ]
    part = take(part, x, 1) + sum(g.astype(f32) for g in got)
    sent = part.astype(b16)
    got = [
        moved(take(sent, (zl + d) % 2, 0), lambda x, y, z, c, d=d: (x, y, z + d, c))
        for d in (2, 1, 3)
    ]
    part = take(part, zl, 0) + sum(g.astype(f32) for g in got)
    sent = part.astype(b16)
    got = [moved(sent, lambda x, y, z, c, d=d: (x, y + d, z, c)) for d in (2, 1, 3)]
    part = part + sum(g.astype(f32) for g in got)
    sent = part.astype(b16)
    got = {d: moved(sent, lambda x, y, z, c, d=d: (x + d, y, z, c)) for d in (2, 1, 3)}
    rel = jnp.stack([sent, got[3], got[2], got[1]])
    rel = jnp.concatenate([rel, rel])
    return lax.dynamic_slice_in_dim(rel, (4 - x) % 4, 4, 0).reshape(288, width).astype(f32)


def on_device(feat, text, head, partner, scale, bias):
    f32, b16 = jnp.float32, jnp.bfloat16
    rows = feat.shape[0]
    feat1 = along_dp(feat, -1)
    text2 = along_dp(text, 2)
    whole = gathered_head(head)
    temper = scale[0]
    offset = bias[0]
    txt_unit, ry = unit_rows(text.astype(f32))
    txt_b = txt_unit.astype(b16)
    txt2_b = unit_rows(text2.astype(f32))[0].astype(b16)
    img0, rx0 = unit_rows(dot32(feat, whole))
    img1, rx1 = unit_rows(dot32(feat1, whole))
    img0_b, img1_b = img0.astype(b16), img1.astype(b16)
    onehot = (partner[:, None] == jnp.arange(rows, dtype=jnp.int32)[None, :]).astype(f32)

    def probability(img_b, txt):
        return jax.nn.sigmoid(temper * dot32(img_b, txt, CONTRACT_COLS) + offset)

    g00 = (probability(img0_b, txt_b) - onehot).astype(b16)
    g02 = probability(img0_b, txt2_b).astype(b16)
    g10 = probability(img1_b, txt_b).astype(b16)
    g12 = probability(img1_b, txt2_b).astype(b16)
    back = dot32(g02, img0_b, CONTRACT_ROWS) + dot32(g12, img1_b, CONTRACT_ROWS)
    back = along_dp(back.astype(b16), -2)

    def projected(img, rx, ga, gb):
        d_img = temper * (dot32(ga, txt_b) + dot32(gb, txt2_b))
        return (rx * (d_img - img * jnp.sum(img * d_img, axis=-1, keepdims=True))).astype(b16)

    part = dot32(feat, projected(img0, rx0, g00, g02), CONTRACT_ROWS)
    part = part + dot32(feat1, projected(img1, rx1, g10, g12), CONTRACT_ROWS)
    head_grad = reduced(part) / rows
    d_txt = dot32(g00, img0_b, CONTRACT_ROWS) + dot32(g10, img1_b, CONTRACT_ROWS)
    d_txt = temper * (d_txt + back.astype(f32))
    text_grad = ry * (d_txt - txt_unit * jnp.sum(txt_unit * d_txt, axis=-1, keepdims=True))
    return (head_grad, text_grad)


def solution(mesh):
    whole = Mesh(mesh.devices.reshape(SIZES), AXES)
    rows = P(AXES, None)
    fsdp = P(("zl", "c"), None)
    return jax.shard_map(
        on_device,
        mesh=whole,
        in_specs=(rows, rows, fsdp, P(AXES), P(), P()),
        out_specs=(fsdp, rows),
        check_vma=False,
    )
```

```python
import functools

import jax
import jax.numpy as jnp
from jax import lax
from jax.experimental import pallas as pl
from jax.experimental.pallas import tpu as pltpu
from jax.sharding import Mesh, PartitionSpec as P

AXES = ("x", "y", "zh", "zl", "c")
SIZES = (4, 4, 2, 2, 2)
ROWS = 768
WIDTH = 1152
BLOCK = 288
HALF = 144
PART = 40
FEATS = (128, 320, 320)
BACKS = (512, 256)
F32 = jnp.float32
B16 = jnp.bfloat16
PLAIN = (((1,), (0,)), ((), ()))
FIRST = (((0,), (0,)), ((), ()))
LAST = (((1,), (1,)), ((), ()))


def index_of(x, y, z, c):
    return ((x % 4 * 4 + y % 4) * 4 + z % 4) * 2 + c


def moved(value, target):
    pairs = [
        (index_of(x, y, z, c), index_of(*target(x, y, z, c)))
        for x in range(4)
        for y in range(4)
        for z in range(4)
        for c in range(2)
    ]
    return lax.ppermute(value, AXES, pairs)


def along_dp(value, by):
    pairs = [(d * 4 + j, (d + by) % 32 * 4 + j) for d in range(32) for j in range(4)]
    return lax.ppermute(value, AXES, pairs)


def to_core(value):
    return moved(value, lambda x, y, z, c: (x, y, z, 1 - c))


def call(kernel, outs, ins, scratch=(), aliases=None, limit=12, work=0, anywhere=(), kept=None):
    specs = [pltpu.SMEM if a.size < 16 else pltpu.VMEM for a in ins]
    out_specs = [pltpu.SMEM if len(s) == 1 else pltpu.VMEM for s, t in outs]
    for k in anywhere:
        specs[k] = pl.ANY
    for k in (kept or {}).values():
        out_specs[k] = pl.ANY
    return pl.pallas_call(
        kernel,
        out_shape=[jax.ShapeDtypeStruct(s, t) for s, t in outs],
        in_specs=[pl.BlockSpec(memory_space=s) for s in specs],
        out_specs=[pl.BlockSpec(memory_space=s) for s in out_specs],
        scratch_shapes=list(scratch),
        input_output_aliases={**(aliases or {}), **(kept or {})},
        cost_estimate=pl.CostEstimate(flops=work, bytes_accessed=0, transcendentals=0),
        compiler_params=pltpu.CompilerParams(vmem_limit_bytes=limit * 1024 * 1024),
    )(*ins)


def cut(arrays, pieces):
    def kernel(*refs):
        ins, outs, sems = refs[: len(arrays)], refs[len(arrays) : -1], refs[-1]
        copies = [
            pltpu.make_async_copy(ins[k].at[pl.ds(at, n)], out, sems.at[i])
            for i, ((k, at, n), out) in enumerate(zip(pieces, outs))
        ]
        for copy in copies:
            copy.start()
        for copy in copies:
            copy.wait()

    return pl.pallas_call(
        kernel,
        out_shape=[jax.ShapeDtypeStruct((n, WIDTH), B16) for _, _, n in pieces],
        in_specs=[pl.BlockSpec(memory_space=pltpu.HBM)] * len(arrays),
        out_specs=[pl.BlockSpec(memory_space=pltpu.HBM)] * len(pieces),
        scratch_shapes=[pltpu.SemaphoreType.DMA((len(pieces),))],
        cost_estimate=pl.CostEstimate(flops=0, bytes_accessed=0, transcendentals=0),
        compiler_params=pltpu.CompilerParams(vmem_limit_bytes=2 * 1024 * 1024),
    )(*arrays)


def gate(value, *after):
    return pl.pallas_call(
        lambda *refs: None,
        out_shape=jax.ShapeDtypeStruct(value.shape, value.dtype),
        in_specs=[pl.BlockSpec(memory_space=pl.ANY)] * (1 + len(after)),
        out_specs=pl.BlockSpec(memory_space=pl.ANY),
        input_output_aliases={0: 0},
        cost_estimate=pl.CostEstimate(flops=0, bytes_accessed=0, transcendentals=0),
        compiler_params=pltpu.CompilerParams(vmem_limit_bytes=2 * 1024 * 1024),
    )(value, *after)


def dot32(a, b, dims=PLAIN):
    return lax.dot_general(a, b, dims, preferred_element_type=F32)


def unit(vec):
    inv = lax.rsqrt(jnp.sum(vec * vec, axis=-1, keepdims=True) + 1e-06)
    return (vec * inv, inv)


def probability(img_b, txt, scale_ref, bias_ref):
    return jax.nn.sigmoid(scale_ref[0] * dot32(img_b, txt, LAST) + bias_ref[0])


def project(feat_ref, whole_ref, img_ref, img_b_ref, rx_ref):
    img, rx = unit(dot32(feat_ref[...], whole_ref[...]))
    img_ref[...] = img
    img_b_ref[...] = img.astype(B16)
    rx_ref[...] = rx


def d_projection(img, rx, d_img, scale):
    d_img = scale[0] * d_img
    inner = jnp.sum(img * d_img, axis=-1, keepdims=True)
    return (rx * (d_img - img * inner)).astype(B16)


def own_kernel(
    index, scale, bias, feat, text, head, up, down, far, far_up, far_down, partner,
    whole, txt_b, img, img_b, rx, grad0, d_img,
):
    zl, c = index[1] % 2, index[2]
    txt_b[...] = unit(text[...].astype(F32))[0].astype(B16)
    near, away = zl * 2, (1 - zl) * 2

    def put(ref, at):
        whole[pl.ds(pl.multiple_of(at, 16), ref.shape[0]), :] = ref[...]

    put(head, (near + c) * BLOCK)
    put(far, (near + 1 - c) * BLOCK)
    put(up, (away + c) * BLOCK)
    put(down, (away + c) * BLOCK + BLOCK // 2)
    put(far_up, (away + 1 - c) * BLOCK)
    put(far_down, (away + 1 - c) * BLOCK + BLOCK // 2)
    project(feat, whole, img, img_b, rx)
    label = lax.broadcasted_iota(jnp.int32, (ROWS, ROWS), 1) == partner[...]
    grad = probability(img_b[...], txt_b[...], scale, bias) - label.astype(F32)
    grad0[...] = grad.astype(B16)
    d_img[...] = dot32(grad0[...], txt_b[...])


def before_kernel(scale, bias, feat, whole, txt_b, img, img_b, rx, grad0, d_img):
    project(feat, whole, img, img_b, rx)
    grad0[...] = probability(img_b[...], txt_b[...], scale, bias).astype(B16)
    d_img[...] = dot32(grad0[...], txt_b[...])


def after(scale, bias, txt2_b, img, img_b, rx, d_img, grad):
    grad[...] = probability(img_b[...], txt2_b[...], scale, bias).astype(B16)
    total = d_img[...] + dot32(grad[...], txt2_b[...])
    return d_projection(img[...], rx[...], total, scale)


def visit_kernel(scale, bias, text2, *refs):
    held = [refs[k : k + 5] for k in (0, 5, 10)]
    txt2_b, *grads, part, feats, d_proj = refs[15:]
    txt2_b[...] = unit(text2[...].astype(F32))[0].astype(B16)
    at = 0
    for (feat, img, img_b, rx, d_img), grad in zip(held, grads):
        rows = pl.ds(at, feat.shape[0])
        feats[rows, :] = feat[...]
        d_proj[rows, :] = after(scale, bias, txt2_b, img, img_b, rx, d_img, grad)
        at += feat.shape[0]
    part[...] = dot32(feats[...], d_proj[...], FIRST)


def last_kernel(
    index, scale, bias, feat, whole, txt_b, txt2_b, part_in,
    img_b, grad0, grad2, keep, send,
    img, rx, d_img, part,
):
    before_kernel(scale, bias, feat, whole, txt_b, img, img_b, rx, grad0, d_img)
    d_proj = after(scale, bias, txt2_b, img, img_b, rx, d_img, grad2)
    part[...] = part_in[...] + dot32(feat[...], d_proj, FIRST)
    c = index[2]
    for zl in range(2):
        rows = pl.ds(zl * BLOCK, BLOCK)
        keep[rows, :] = part[pl.ds(pl.multiple_of((zl * 2 + c) * BLOCK, 8), BLOCK), :]
        gone = part[pl.ds(pl.multiple_of((zl * 2 + 1 - c) * BLOCK, 8), BLOCK), :]
        send[rows, :] = gone.astype(B16)


def text_sum(grads, imgs):
    total = dot32(grads[0][...], imgs[0][...], FIRST)
    for grad, img in zip(grads[1:], imgs[1:]):
        total = total + dot32(grad[...], img[...], FIRST)
    return total


def back_kernel(at, n, *refs):
    grads = [grad.at[:, at : at + n] for grad in refs[:4]]
    refs[8][...] = text_sum(grads, refs[4:8]).astype(B16)


def text_kernel(*refs):
    refs[8][...] = text_sum(refs[:4], refs[4:8])


def end_kernel(at, scale, text, d_txt_in, back, *refs):
    out, rows, sem = refs[-3:]
    n = rows.shape[0]
    txt, ry = unit(text[at : at + n, :].astype(F32))
    d_txt = scale[0] * (d_txt_in[at : at + n, :] + back[...].astype(F32))
    inner = jnp.sum(txt * d_txt, axis=-1, keepdims=True)
    rows[...] = ry * (d_txt - txt * inner)
    copy = pltpu.make_async_copy(rows, out.at[pl.ds(at, n)], sem)
    copy.start()
    copy.wait()


def core_sum_kernel(index, keep, got, own, to1, to2, to3, total):
    total[...] = keep[...] + got[...].astype(F32)
    for d, ref in enumerate((own, to1, to2, to3)):
        z = (index[1] + d) % 4
        zl = z % 2
        at = pl.multiple_of(zl * BLOCK + z // 2 * HALF, 8)
        ref[...] = total[pl.ds(at, HALF), :].astype(ref.dtype)


def summed(own, *gots):
    value = own[...]
    for got in gots:
        value = value + got[...].astype(F32)
    return value


def z_sum_kernel(index, own, got1, got2, got3, mine, to1, to2, to3, total):
    x = index[0]
    total[HALF:, :] = jnp.zeros_like(total[HALF:, :])
    total[:HALF, :] = summed(own, got1, got2, got3)
    for d, ref in enumerate((mine, to1, to2, to3)):
        at = pl.multiple_of((x + d) % 4 * PART, 8)
        ref[...] = total[pl.ds(at, PART), :].astype(ref.dtype)


def x_sum_kernel(own, got1, got2, got3, came, held, total, send, passed):
    value = summed(own, got1, got2, got3)
    total[...] = value
    send[...] = value.astype(B16)


def y_sum_kernel(own, got1, got2, got3, send):
    send[...] = (summed(own, got1, got2, got3) / ROWS).astype(B16)


def pair_kernel(index, own, got, pair):
    zh = index[1] // 2
    pair[0] = jnp.where(zh == 0, own[...], got[...])
    pair[1] = jnp.where(zh == 0, got[...], own[...])


def gather_kernel(index, own, got1, got2, got3, out):
    for d, ref in enumerate((own, got1, got2, got3)):
        x = (index[0] + 4 - d) % 4
        for zh in range(2):
            value = ref[zh].astype(F32)
            at = pl.multiple_of(zh * HALF + x * PART, 8)

            @pl.when(x < 3)
            def _():
                out[pl.ds(at, PART), :] = value

            @pl.when(x == 3)
            def _():
                out[pl.ds(at, HALF - 3 * PART), :] = value[: HALF - 3 * PART, :]


def on_device(feat, text, head, partner, scale, bias):
    z = lax.axis_index("zh") * 2 + lax.axis_index("zl")
    index = jnp.stack([lax.axis_index("x"), z, lax.axis_index("c")]).astype(jnp.int32)
    half = BLOCK // 2

    top, bottom = cut([head], [(0, 0, half), (0, half, half)])
    up = moved(top, lambda x, y, z, c: (x, y, z - 1, c))
    down = moved(bottom, lambda x, y, z, c: (x, y, z + 1, c))
    text2 = along_dp(text, 2)
    n_a, n_b, n_c = FEATS
    feat_a, feat_b, feat_c = cut([feat], [(0, 0, n_a), (0, n_a, n_b), (0, n_a + n_b, n_c)])
    feat1a, feat1b = along_dp(feat_a, -1), along_dp(gate(feat_b, up, down), -1)
    far, far_up, far_down = to_core(head), to_core(gate(up, feat1a)), to_core(down)

    full = (ROWS, WIDTH)
    square = (WIDTH, WIDTH)
    whole, txt_b, img, img_b, rx, grad0, d_img = call(
        own_kernel,
        [(square, B16), (full, B16), (full, F32), (full, B16), ((ROWS, 1), F32)]
        + [((ROWS, ROWS), B16), (full, F32)],
        [index, scale, bias, feat, text, head, up, down, far, far_up, far_down]
        + [partner.reshape(ROWS, 1)],
        work=0,
    )
    feat1c = along_dp(gate(feat_c, txt_b), -1)
    held, grads0 = [feat, img, img_b, rx, d_img], [grad0]
    imgs = [img_b]
    for feat1 in (feat1a, feat1b):
        n = feat1.shape[0]
        img, img_b, rx, grad0, d_img = call(
            before_kernel,
            [((n, WIDTH), F32), ((n, WIDTH), B16), ((n, 1), F32), ((n, ROWS), B16)]
            + [((n, WIDTH), F32)],
            [scale, bias, feat1, whole, txt_b],
        )
        held += [feat1, img, img_b, rx, d_img]
        grads0 += [grad0]
        imgs += [img_b]
    txt2_b, *grads2, part = call(
        visit_kernel,
        [(full, B16)] + [((n, ROWS), B16) for n in (ROWS, n_a, n_b)] + [(square, F32)],
        [scale, bias, text2, *held],
        scratch=[pltpu.VMEM((ROWS + n_a + n_b, WIDTH), B16)] * 2,
        limit=20,
    )
    last = (n_c, WIDTH)
    img_b, grad0, grad2, keep, send = call(
        last_kernel,
        [(last, B16), ((n_c, ROWS), B16), ((n_c, ROWS), B16)]
        + [((2 * BLOCK, WIDTH), F32), ((2 * BLOCK, WIDTH), B16)],
        [index, scale, bias, feat1c, whole, txt_b, txt2_b, part],
        scratch=[
            pltpu.VMEM(last, F32), pltpu.VMEM((n_c, 1), F32),
            pltpu.VMEM(last, F32), pltpu.VMEM(square, F32),
        ],
        limit=14,
    )
    grads0, grads2, imgs = grads0 + [grad0], grads2 + [grad2], imgs + [img_b]

    def back_rows(at, n):
        (rows,) = call(
            functools.partial(back_kernel, at, n), [((n, WIDTH), B16)], [*grads2, *imgs]
        )
        return rows

    got = to_core(send)
    back_a = along_dp(back_rows(0, BACKS[0]), -2)
    half = (HALF, WIDTH)
    small = (PART, WIDTH)
    own, *sends = call(
        core_sum_kernel,
        [(half, F32)] + [(half, B16)] * 3,
        [index, keep, got],
        scratch=[pltpu.VMEM((2 * BLOCK, WIDTH), F32)],
    )
    gots = [moved(sends[d - 1], lambda x, y, z, c, d=d: (x, y, z + d, c)) for d in (1, 2, 3)]
    own, *sends = call(
        z_sum_kernel,
        [(small, F32)] + [(small, B16)] * 3,
        [index, own, *gots],
        scratch=[pltpu.VMEM((4 * PART, WIDTH), F32)],
    )
    gots = [moved(sends[d - 1], lambda x, y, z, c, d=d: (x + d, y, z, c)) for d in (1, 2, 3)]
    back_b = back_rows(*BACKS)
    own, send, back_b = call(
        x_sum_kernel,
        [(small, F32), (small, B16), (back_b.shape, B16)],
        [own, *gots, back_a, back_b],
        anywhere=(4, 5),
        kept={5: 2},
        work=0,
    )
    gots = [moved(send, lambda x, y, z, c, d=d: (x, y + d, z, c)) for d in (1, 2, 3)]
    back_b = along_dp(back_b, -2)
    (send,) = call(y_sum_kernel, [(small, B16)], [own, *gots], work=5 * 10**9)
    got = moved(send, lambda x, y, z, c: (x, y, z + 2, c))
    (pair,) = call(pair_kernel, [((2, *small), B16)], [index, send, got])
    gots = [moved(pair, lambda x, y, z, c, d=d: (x + d, y, z, c)) for d in (1, 2, 3)]
    (head_grad,) = call(
        gather_kernel, [((BLOCK, WIDTH), F32)], [index, pair, *gots], work=0
    )

    (d_txt,) = call(text_kernel, [(full, F32)], [*grads0, *imgs])
    text_grad = None
    for at, back in ((0, back_a), (BACKS[0], back_b)):
        before = [] if text_grad is None else [text_grad]
        text_grad = pl.pallas_call(
            functools.partial(end_kernel, at),
            out_shape=jax.ShapeDtypeStruct(full, F32),
            in_specs=[pl.BlockSpec(memory_space=pltpu.SMEM)]
            + [pl.BlockSpec(memory_space=pltpu.VMEM)] * 3
            + [pl.BlockSpec(memory_space=pl.ANY)] * len(before),
            out_specs=pl.BlockSpec(memory_space=pl.ANY),
            scratch_shapes=[pltpu.VMEM(back.shape, F32), pltpu.SemaphoreType.DMA],
            input_output_aliases={4: 0} if before else {},
            compiler_params=pltpu.CompilerParams(vmem_limit_bytes=12 * 1024 * 1024),
        )(scale, text, d_txt, back, *before)
    return (head_grad, text_grad)


def solution(mesh):
    whole = Mesh(mesh.devices.reshape(SIZES), AXES)
    rows = P(AXES, None)
    fsdp = P(("zl", "c"), None)
    return jax.shard_map(
        on_device,
        mesh=whole,
        in_specs=(rows, rows, fsdp, P(AXES), P(), P()),
        out_specs=(fsdp, rows),
        check_vma=False,
    )
```

```python
import functools

import jax
import jax.numpy as jnp
from jax import lax
from jax.experimental import pallas as pl
from jax.experimental.pallas import tpu as pltpu
from jax.sharding import Mesh, PartitionSpec as P

AXES = ("x", "y", "zh", "zl", "c")
SIZES = (4, 4, 2, 2, 2)
ROWS = 768
WIDTH = 1152
BLOCK = 288
HALF = 144
PART = 40
FEATS = (288, 256, 224)
BACKS = (512, 256)
F32 = jnp.float32
B16 = jnp.bfloat16
PLAIN = (((1,), (0,)), ((), ()))
FIRST = (((0,), (0,)), ((), ()))
LAST = (((1,), (1,)), ((), ()))


def index_of(x, y, z, c):
    return ((x % 4 * 4 + y % 4) * 4 + z % 4) * 2 + c


def moved(value, target):
    pairs = [
        (index_of(x, y, z, c), index_of(*target(x, y, z, c)))
        for x in range(4)
        for y in range(4)
        for z in range(4)
        for c in range(2)
    ]
    return lax.ppermute(value, AXES, pairs)


def along_dp(value, by):
    pairs = [(d * 4 + j, (d + by) % 32 * 4 + j) for d in range(32) for j in range(4)]
    return lax.ppermute(value, AXES, pairs)


def to_core(value):
    return moved(value, lambda x, y, z, c: (x, y, z, 1 - c))


def call(kernel, outs, ins, scratch=(), aliases=None, limit=12, work=0, anywhere=(), kept=None):
    specs = [pltpu.SMEM if a.size < 16 else pltpu.VMEM for a in ins]
    out_specs = [pltpu.SMEM if len(s) == 1 else pltpu.VMEM for s, t in outs]
    for k in anywhere:
        specs[k] = pl.ANY
    for k in (kept or {}).values():
        out_specs[k] = pl.ANY
    return pl.pallas_call(
        kernel,
        out_shape=[jax.ShapeDtypeStruct(s, t) for s, t in outs],
        in_specs=[pl.BlockSpec(memory_space=s) for s in specs],
        out_specs=[pl.BlockSpec(memory_space=s) for s in out_specs],
        scratch_shapes=list(scratch),
        input_output_aliases={**(aliases or {}), **(kept or {})},
        cost_estimate=pl.CostEstimate(flops=work, bytes_accessed=0, transcendentals=0),
        compiler_params=pltpu.CompilerParams(vmem_limit_bytes=limit * 1024 * 1024),
    )(*ins)


def cut(arrays, pieces):
    def kernel(*refs):
        ins, outs, sems = refs[: len(arrays)], refs[len(arrays) : -1], refs[-1]
        copies = [
            pltpu.make_async_copy(ins[k].at[pl.ds(at, n)], out, sems.at[i])
            for i, ((k, at, n), out) in enumerate(zip(pieces, outs))
        ]
        for copy in copies:
            copy.start()
        for copy in copies:
            copy.wait()

    return pl.pallas_call(
        kernel,
        out_shape=[jax.ShapeDtypeStruct((n, WIDTH), B16) for _, _, n in pieces],
        in_specs=[pl.BlockSpec(memory_space=pl.ANY)] * len(arrays),
        out_specs=[pl.BlockSpec(memory_space=pl.ANY)] * len(pieces),
        scratch_shapes=[pltpu.SemaphoreType.DMA((len(pieces),))],
        cost_estimate=pl.CostEstimate(flops=0, bytes_accessed=0, transcendentals=0),
        compiler_params=pltpu.CompilerParams(vmem_limit_bytes=2 * 1024 * 1024),
    )(*arrays)


def gate(values, *after):
    n = len(values)
    return pl.pallas_call(
        lambda *refs: None,
        out_shape=[jax.ShapeDtypeStruct(v.shape, v.dtype) for v in values],
        in_specs=[
            pl.BlockSpec(memory_space=pltpu.SMEM if v.size == 1 else pl.ANY)
            for v in (*values, *after)
        ],
        out_specs=[pl.BlockSpec(memory_space=pl.ANY)] * n,
        input_output_aliases={k: k for k in range(n)},
        cost_estimate=pl.CostEstimate(flops=0, bytes_accessed=0, transcendentals=0),
        compiler_params=pltpu.CompilerParams(vmem_limit_bytes=2 * 1024 * 1024),
    )(*values, *after)


def dot32(a, b, dims=PLAIN):
    return lax.dot_general(a, b, dims, preferred_element_type=F32)


def unit(vec):
    inv = lax.rsqrt(jnp.sum(vec * vec, axis=-1, keepdims=True) + 1e-06)
    return (vec * inv, inv)


def probability(img_b, txt, scale_ref, bias_ref):
    return jax.nn.sigmoid(scale_ref[0] * dot32(img_b, txt, LAST) + bias_ref[0])


def project(feat_ref, whole_ref, img_ref, img_b_ref, rx_ref):
    img, rx = unit(dot32(feat_ref[...], whole_ref[...]))
    img_ref[...] = img
    img_b_ref[...] = img.astype(B16)
    rx_ref[...] = rx


def d_projection(img, rx, d_img, scale):
    d_img = scale[0] * d_img
    inner = jnp.sum(img * d_img, axis=-1, keepdims=True)
    return (rx * (d_img - img * inner)).astype(B16)


def prepare_kernel(
    index, feat, text, head, far, partner, txt_b, near, who, feat_a, feat_b, feat_c, done
):
    c = index[2]
    txt_b[...] = unit(text[...].astype(F32))[0].astype(B16)
    near[pl.ds(pl.multiple_of(c * BLOCK, 16), BLOCK), :] = head[...]
    near[pl.ds(pl.multiple_of((1 - c) * BLOCK, 16), BLOCK), :] = far[...]
    who[...] = partner[...]
    at = 0
    for piece in (feat_a, feat_b, feat_c):
        piece[...] = feat[at : at + piece.shape[0], :]
        at += piece.shape[0]
    done[0] = 0


def own_kernel(
    index, scale, bias, feat, txt_b, near, up, down, far_up, far_down, who,
    whole, img, img_b, rx, grad0, d_img,
):
    zl, c = index[1] % 2, index[2]
    away = (1 - zl) * 2

    def put(ref, at):
        whole[pl.ds(pl.multiple_of(at, 16), ref.shape[0]), :] = ref[...]

    put(near, zl * 2 * BLOCK)
    put(up, (away + c) * BLOCK)
    put(down, (away + c) * BLOCK + BLOCK // 2)
    put(far_up, (away + 1 - c) * BLOCK)
    put(far_down, (away + 1 - c) * BLOCK + BLOCK // 2)
    project(feat, whole, img, img_b, rx)
    label = lax.broadcasted_iota(jnp.int32, (ROWS, ROWS), 1) == who[...]
    grad = probability(img_b[...], txt_b[...], scale, bias) - label.astype(F32)
    grad0[...] = grad.astype(B16)
    d_img[...] = dot32(grad0[...], txt_b[...])


def before_kernel(scale, bias, feat, whole, txt_b, img, img_b, rx, grad0, d_img):
    project(feat, whole, img, img_b, rx)
    grad0[...] = probability(img_b[...], txt_b[...], scale, bias).astype(B16)
    d_img[...] = dot32(grad0[...], txt_b[...])


def after(scale, bias, txt2_b, img, img_b, rx, d_img, grad):
    grad[...] = probability(img_b[...], txt2_b[...], scale, bias).astype(B16)
    total = d_img[...] + dot32(grad[...], txt2_b[...])
    return d_projection(img[...], rx[...], total, scale)


def visit_kernel(
    scale, bias, text2, img, img_b, rx, d_img, img1, img1_b, rx1, d_img1,
    txt2_b, grad, d_proj, grad1, d_proj1,
):
    txt2_b[...] = unit(text2[...].astype(F32))[0].astype(B16)
    d_proj[...] = after(scale, bias, txt2_b, img, img_b, rx, d_img, grad)
    d_proj1[...] = after(scale, bias, txt2_b, img1, img1_b, rx1, d_img1, grad1)


def second_kernel(
    scale, bias, feat, whole, txt_b, txt2_b, feat0, d_proj0, feat1, d_proj1,
    img_b, grad0, grad2, part,
    img, rx, d_img, feats, d_proj,
):
    before_kernel(scale, bias, feat, whole, txt_b, img, img_b, rx, grad0, d_img)
    d_proj[ROWS + FEATS[0] :, :] = after(scale, bias, txt2_b, img, img_b, rx, d_img, grad2)
    for at, rows, grad in ((0, feat0, d_proj0), (ROWS, feat1, d_proj1)):
        feats[at : at + rows.shape[0], :] = rows[...]
        d_proj[at : at + rows.shape[0], :] = grad[...]
    feats[ROWS + FEATS[0] :, :] = feat[...]
    part[...] = dot32(feats[...], d_proj[...], FIRST)


def last_kernel(
    index, scale, bias, feat, whole, txt_b, txt2_b, part_in,
    img_b, grad0, grad2, keep, send,
    img, rx, d_img, part,
):
    before_kernel(scale, bias, feat, whole, txt_b, img, img_b, rx, grad0, d_img)
    d_proj = after(scale, bias, txt2_b, img, img_b, rx, d_img, grad2)
    part[...] = part_in[...] + dot32(feat[...], d_proj, FIRST)
    c = index[2]
    for zl in range(2):
        rows = pl.ds(zl * BLOCK, BLOCK)
        keep[rows, :] = part[pl.ds(pl.multiple_of((zl * 2 + c) * BLOCK, 8), BLOCK), :]
        gone = part[pl.ds(pl.multiple_of((zl * 2 + 1 - c) * BLOCK, 8), BLOCK), :]
        send[rows, :] = gone.astype(B16)


def text_sum(grads, imgs):
    total = dot32(grads[0][...], imgs[0][...], FIRST)
    for grad, img in zip(grads[1:], imgs[1:]):
        total = total + dot32(grad[...], img[...], FIRST)
    return total


def back_kernel(at, n, *refs):
    grads = [grad.at[:, at : at + n] for grad in refs[:4]]
    refs[8][...] = text_sum(grads, refs[4:8]).astype(B16)


def text_kernel(*refs):
    refs[8][...] = text_sum(refs[:4], refs[4:8])
    refs[9][0] = 0


def end_kernel(at, scale, text, d_txt_in, back, *refs):
    out, done, rows, sem = refs[-4:]
    n = rows.shape[0]
    txt, ry = unit(text[at : at + n, :].astype(F32))
    d_txt = scale[0] * (d_txt_in[at : at + n, :] + back[...].astype(F32))
    inner = jnp.sum(txt * d_txt, axis=-1, keepdims=True)
    rows[...] = ry * (d_txt - txt * inner)
    copy = pltpu.make_async_copy(rows, out.at[pl.ds(at, n)], sem)
    copy.start()
    copy.wait()
    done[0] = 0


def core_sum_kernel(index, keep, got, own, to1, to2, to3, total):
    total[...] = keep[...] + got[...].astype(F32)
    for d, ref in enumerate((own, to1, to2, to3)):
        z = (index[1] + d) % 4
        zl = z % 2
        at = pl.multiple_of(zl * BLOCK + z // 2 * HALF, 8)
        ref[...] = total[pl.ds(at, HALF), :].astype(ref.dtype)


def summed(own, *gots):
    value = own[...]
    for got in gots:
        value = value + got[...].astype(F32)
    return value


def z_sum_kernel(index, own, got1, got2, got3, done, mine, to1, to2, to3, total):
    x = index[0]
    total[HALF:, :] = jnp.zeros_like(total[HALF:, :])
    total[:HALF, :] = summed(own, got1, got2, got3)
    for d, ref in enumerate((mine, to1, to2, to3)):
        at = pl.multiple_of((x + d) % 4 * PART, 8)
        ref[...] = total[pl.ds(at, PART), :].astype(ref.dtype)


def x_sum_kernel(own, got1, got2, got3, came, held, total, send, passed):
    value = summed(own, got1, got2, got3)
    total[...] = value
    send[...] = value.astype(B16)


def y_sum_kernel(own, got1, got2, got3, send):
    send[...] = (summed(own, got1, got2, got3) / ROWS).astype(B16)


def pair_kernel(index, own, got, done, pair):
    zh = index[1] // 2
    pair[0] = jnp.where(zh == 0, own[...], got[...])
    pair[1] = jnp.where(zh == 0, got[...], own[...])


def gather_kernel(index, own, got1, got2, got3, after, out):
    for d, ref in enumerate((own, got1, got2, got3)):
        x = (index[0] + 4 - d) % 4
        for zh in range(2):
            value = ref[zh].astype(F32)
            at = pl.multiple_of(zh * HALF + x * PART, 8)

            @pl.when(x < 3)
            def _():
                out[pl.ds(at, PART), :] = value

            @pl.when(x == 3)
            def _():
                out[pl.ds(at, HALF - 3 * PART), :] = value[: HALF - 3 * PART, :]


def on_device(feat, text, head, partner, scale, bias):
    z = lax.axis_index("zh") * 2 + lax.axis_index("zl")
    index = jnp.stack([lax.axis_index("x"), z, lax.axis_index("c")]).astype(jnp.int32)
    half = BLOCK // 2

    n_a, n_b, n_c = FEATS
    top, bottom = cut([head], [(0, 0, half), (0, half, half)])
    text2 = along_dp(text, 2)
    up = moved(top, lambda x, y, z, c: (x, y, z - 1, c))
    down = moved(bottom, lambda x, y, z, c: (x, y, z + 1, c))
    far = to_core(head)
    full = (ROWS, WIDTH)
    square = (WIDTH, WIDTH)
    txt_b, near, who, feat_a, feat_b, feat_c, done = call(
        prepare_kernel,
        [(full, B16), ((2 * BLOCK, WIDTH), B16), ((ROWS, 1), jnp.int32)]
        + [((n, WIDTH), B16) for n in FEATS]
        + [((1,), jnp.int32)],
        [index, feat, text, head, far, partner.reshape(ROWS, 1)],
        limit=6,
        work=0,
    )
    up, down, feat_a, feat_b = gate([up, down, feat_a, feat_b], done)
    far_up, far_down = to_core(up), to_core(down)
    feat1a, feat1b = along_dp(feat_a, -1), along_dp(feat_b, -1)
    whole, img, img_b, rx, grad0, d_img = call(
        own_kernel,
        [(square, B16), (full, F32), (full, B16), ((ROWS, 1), F32)]
        + [((ROWS, ROWS), B16), (full, F32)],
        [index, scale, bias, feat, txt_b, near, up, down, far_up, far_down, who],
        work=0,
    )
    (feat_c,) = gate([feat_c], rx)
    feat1c = along_dp(feat_c, -1)
    first = (n_a, WIDTH)
    img1, img1_b, rx1, grad10, d_img1 = call(
        before_kernel,
        [(first, F32), (first, B16), ((n_a, 1), F32), ((n_a, ROWS), B16), (first, F32)],
        [scale, bias, feat1a, whole, txt_b],
    )
    txt2_b, grad2, d_proj, grad12, d_proj1 = call(
        visit_kernel,
        [(full, B16), ((ROWS, ROWS), B16), (full, B16), ((n_a, ROWS), B16), (first, B16)],
        [scale, bias, text2, img, img_b, rx, d_img, img1, img1_b, rx1, d_img1],
    )
    held = (ROWS + n_a + n_b, WIDTH)
    second = (n_b, WIDTH)
    img2_b, grad20, grad22, part = call(
        second_kernel,
        [(second, B16), ((n_b, ROWS), B16), ((n_b, ROWS), B16), (square, F32)],
        [scale, bias, feat1b, whole, txt_b, txt2_b, feat, d_proj, feat1a, d_proj1],
        scratch=[pltpu.VMEM(second, F32), pltpu.VMEM((n_b, 1), F32), pltpu.VMEM(second, F32)]
        + [pltpu.VMEM(held, B16), pltpu.VMEM(held, B16)],
        limit=18,
    )
    grads0, grads2, imgs = [grad0, grad10, grad20], [grad2, grad12, grad22], [img_b, img1_b, img2_b]
    last = (n_c, WIDTH)
    img_b, grad0, grad2, keep, send = call(
        last_kernel,
        [(last, B16), ((n_c, ROWS), B16), ((n_c, ROWS), B16)]
        + [((2 * BLOCK, WIDTH), F32), ((2 * BLOCK, WIDTH), B16)],
        [index, scale, bias, feat1c, whole, txt_b, txt2_b, part],
        scratch=[
            pltpu.VMEM(last, F32), pltpu.VMEM((n_c, 1), F32),
            pltpu.VMEM(last, F32), pltpu.VMEM(square, F32),
        ],
        limit=14,
    )
    grads0, grads2, imgs = grads0 + [grad0], grads2 + [grad2], imgs + [img_b]

    def back_rows(at, n):
        (rows,) = call(
            functools.partial(back_kernel, at, n), [((n, WIDTH), B16)], [*grads2, *imgs]
        )
        return rows

    got = to_core(send)
    d_txt, done = call(
        text_kernel, [(full, F32), ((1,), jnp.int32)], [*grads0, *imgs]
    )
    back_a = along_dp(back_rows(0, BACKS[0]), -2)
    half = (HALF, WIDTH)
    small = (PART, WIDTH)
    own, *sends = call(
        core_sum_kernel,
        [(half, F32)] + [(half, B16)] * 3,
        [index, keep, got],
        scratch=[pltpu.VMEM((2 * BLOCK, WIDTH), F32)],
    )
    gots = [moved(sends[d - 1], lambda x, y, z, c, d=d: (x, y, z + d, c)) for d in (1, 2, 3)]
    own, *sends = call(
        z_sum_kernel,
        [(small, F32)] + [(small, B16)] * 3,
        [index, own, *gots, done],
        scratch=[pltpu.VMEM((4 * PART, WIDTH), F32)],
    )
    gots = [moved(sends[d - 1], lambda x, y, z, c, d=d: (x + d, y, z, c)) for d in (1, 2, 3)]
    back_b = back_rows(*BACKS)
    own, send, back_b = call(
        x_sum_kernel,
        [(small, F32), (small, B16), (back_b.shape, B16)],
        [own, *gots, back_a, back_b],
        anywhere=(4, 5),
        kept={5: 2},
        work=0,
    )
    gots = [moved(send, lambda x, y, z, c, d=d: (x, y + d, z, c)) for d in (1, 2, 3)]
    back_b = along_dp(back_b, -2)
    (send,) = call(y_sum_kernel, [(small, B16)], [own, *gots], work=5 * 10**9)
    got = moved(send, lambda x, y, z, c: (x, y, z + 2, c))

    def end_rows(at, back, *before):
        return pl.pallas_call(
            functools.partial(end_kernel, at),
            out_shape=[
                jax.ShapeDtypeStruct(full, F32), jax.ShapeDtypeStruct((1,), jnp.int32)
            ],
            in_specs=[pl.BlockSpec(memory_space=pltpu.SMEM)]
            + [pl.BlockSpec(memory_space=pltpu.VMEM)] * 3
            + [pl.BlockSpec(memory_space=pl.ANY)] * len(before),
            out_specs=[
                pl.BlockSpec(memory_space=pl.ANY), pl.BlockSpec(memory_space=pltpu.SMEM)
            ],
            scratch_shapes=[pltpu.VMEM(back.shape, F32), pltpu.SemaphoreType.DMA],
            input_output_aliases={4: 0} if before else {},
            compiler_params=pltpu.CompilerParams(vmem_limit_bytes=12 * 1024 * 1024),
        )(scale, text, d_txt, back, *before)

    text_grad, done = end_rows(0, back_a)
    (pair,) = call(pair_kernel, [((2, *small), B16)], [index, send, got, done])
    gots = [moved(pair, lambda x, y, z, c, d=d: (x + d, y, z, c)) for d in (1, 2, 3)]
    text_grad, done = end_rows(BACKS[0], back_b, text_grad)
    (head_grad,) = call(
        gather_kernel,
        [((BLOCK, WIDTH), F32)],
        [index, pair, *gots, done],
        work=0,
    )
    return (head_grad, text_grad)


def solution(mesh):
    whole = Mesh(mesh.devices.reshape(SIZES), AXES)
    rows = P(AXES, None)
    fsdp = P(("zl", "c"), None)
    return jax.shard_map(
        on_device,
        mesh=whole,
        in_specs=(rows, rows, fsdp, P(AXES), P(), P()),
        out_specs=(fsdp, rows),
        check_vma=False,
    )
```

```python
import functools

import jax
import jax.numpy as jnp
from jax import lax
from jax.experimental import pallas as pl
from jax.experimental.pallas import tpu as pltpu
from jax.sharding import Mesh, PartitionSpec as P

AXES = ("x", "y", "zh", "zl", "c")
SIZES = (4, 4, 2, 2, 2)
ROWS = 768
WIDTH = 1152
BLOCK = 288
HALF = 144
PART = 40
FEATS = (288, 256, 224)
BACKS = (512, 256)
F32 = jnp.float32
B16 = jnp.bfloat16
PLAIN = (((1,), (0,)), ((), ()))
FIRST = (((0,), (0,)), ((), ()))
LAST = (((1,), (1,)), ((), ()))


def index_of(x, y, z, c):
    return ((x % 4 * 4 + y % 4) * 4 + z % 4) * 2 + c


def moved(value, target):
    pairs = [
        (index_of(x, y, z, c), index_of(*target(x, y, z, c)))
        for x in range(4)
        for y in range(4)
        for z in range(4)
        for c in range(2)
    ]
    return lax.ppermute(value, AXES, pairs)


def along_dp(value, by):
    pairs = [(d * 4 + j, (d + by) % 32 * 4 + j) for d in range(32) for j in range(4)]
    return lax.ppermute(value, AXES, pairs)


def to_core(value):
    return moved(value, lambda x, y, z, c: (x, y, z, 1 - c))


def call(kernel, outs, ins, scratch=(), aliases=None, limit=12, work=0, anywhere=(), kept=None):
    specs = [pltpu.SMEM if a.size < 16 else pltpu.VMEM for a in ins]
    out_specs = [pltpu.SMEM if len(s) == 1 else pltpu.VMEM for s, t in outs]
    for k in anywhere:
        specs[k] = pl.ANY
    for k in (kept or {}).values():
        out_specs[k] = pl.ANY
    return pl.pallas_call(
        kernel,
        out_shape=[jax.ShapeDtypeStruct(s, t) for s, t in outs],
        in_specs=[pl.BlockSpec(memory_space=s) for s in specs],
        out_specs=[pl.BlockSpec(memory_space=s) for s in out_specs],
        scratch_shapes=list(scratch),
        input_output_aliases={**(aliases or {}), **(kept or {})},
        cost_estimate=pl.CostEstimate(flops=work, bytes_accessed=0, transcendentals=0),
        compiler_params=pltpu.CompilerParams(vmem_limit_bytes=limit * 1024 * 1024),
    )(*ins)


def cut(arrays, pieces):
    def kernel(*refs):
        ins, outs, sems = refs[: len(arrays)], refs[len(arrays) : -1], refs[-1]
        copies = [
            pltpu.make_async_copy(ins[k].at[pl.ds(at, n)], out, sems.at[i])
            for i, ((k, at, n), out) in enumerate(zip(pieces, outs))
        ]
        for copy in copies:
            copy.start()
        for copy in copies:
            copy.wait()

    return pl.pallas_call(
        kernel,
        out_shape=[jax.ShapeDtypeStruct((n, WIDTH), B16) for _, _, n in pieces],
        in_specs=[pl.BlockSpec(memory_space=pl.ANY)] * len(arrays),
        out_specs=[pl.BlockSpec(memory_space=pl.ANY)] * len(pieces),
        scratch_shapes=[pltpu.SemaphoreType.DMA((len(pieces),))],
        cost_estimate=pl.CostEstimate(flops=0, bytes_accessed=0, transcendentals=0),
        compiler_params=pltpu.CompilerParams(vmem_limit_bytes=2 * 1024 * 1024),
    )(*arrays)


def gate(values, *after):
    n = len(values)
    return pl.pallas_call(
        lambda *refs: None,
        out_shape=[jax.ShapeDtypeStruct(v.shape, v.dtype) for v in values],
        in_specs=[
            pl.BlockSpec(memory_space=pltpu.SMEM if v.size == 1 else pl.ANY)
            for v in (*values, *after)
        ],
        out_specs=[pl.BlockSpec(memory_space=pl.ANY)] * n,
        input_output_aliases={k: k for k in range(n)},
        cost_estimate=pl.CostEstimate(flops=0, bytes_accessed=0, transcendentals=0),
        compiler_params=pltpu.CompilerParams(vmem_limit_bytes=2 * 1024 * 1024),
    )(*values, *after)


def dot32(a, b, dims=PLAIN):
    return lax.dot_general(a, b, dims, preferred_element_type=F32)


def unit(vec):
    inv = lax.rsqrt(jnp.sum(vec * vec, axis=-1, keepdims=True) + 1e-06)
    return (vec * inv, inv)


def probability(img_b, txt, scale_ref, bias_ref):
    return jax.nn.sigmoid(scale_ref[0] * dot32(img_b, txt, LAST) + bias_ref[0])


def project(feat_ref, whole_ref, img_ref, img_b_ref, rx_ref):
    img, rx = unit(dot32(feat_ref[...], whole_ref[...]))
    img_ref[...] = img
    img_b_ref[...] = img.astype(B16)
    rx_ref[...] = rx


def d_projection(img, rx, d_img, scale):
    d_img = scale[0] * d_img
    inner = jnp.sum(img * d_img, axis=-1, keepdims=True)
    return (rx * (d_img - img * inner)).astype(B16)


def prepare_kernel(
    index, feat, text, head, far, partner, txt_b, near, who, feat_a, feat_b, feat_c, done
):
    c = index[2]
    txt_b[...] = unit(text[...].astype(F32))[0].astype(B16)
    near[pl.ds(pl.multiple_of(c * BLOCK, 16), BLOCK), :] = head[...]
    near[pl.ds(pl.multiple_of((1 - c) * BLOCK, 16), BLOCK), :] = far[...]
    who[...] = partner[...]
    at = 0
    for piece in (feat_a, feat_b, feat_c):
        piece[...] = feat[at : at + piece.shape[0], :]
        at += piece.shape[0]
    done[0] = 0


def own_kernel(
    index, scale, bias, feat, txt_b, near, up, down, far_up, far_down, who,
    whole, img, img_b, rx, grad0, d_img,
):
    zl, c = index[1] % 2, index[2]
    away = (1 - zl) * 2

    def put(ref, at):
        whole[pl.ds(pl.multiple_of(at, 16), ref.shape[0]), :] = ref[...]

    put(near, zl * 2 * BLOCK)
    put(up, (away + c) * BLOCK)
    put(down, (away + c) * BLOCK + BLOCK // 2)
    put(far_up, (away + 1 - c) * BLOCK)
    put(far_down, (away + 1 - c) * BLOCK + BLOCK // 2)
    project(feat, whole, img, img_b, rx)
    label = lax.broadcasted_iota(jnp.int32, (ROWS, ROWS), 1) == who[...]
    grad = probability(img_b[...], txt_b[...], scale, bias) - label.astype(F32)
    grad0[...] = grad.astype(B16)
    d_img[...] = dot32(grad0[...], txt_b[...])


def before_kernel(scale, bias, feat, whole, txt_b, img, img_b, rx, grad0, d_img):
    project(feat, whole, img, img_b, rx)
    grad0[...] = probability(img_b[...], txt_b[...], scale, bias).astype(B16)
    d_img[...] = dot32(grad0[...], txt_b[...])


def after(scale, bias, txt2_b, img, img_b, rx, d_img, grad):
    grad[...] = probability(img_b[...], txt2_b[...], scale, bias).astype(B16)
    total = d_img[...] + dot32(grad[...], txt2_b[...])
    return d_projection(img[...], rx[...], total, scale)


def visit_kernel(
    scale, bias, text2, img, img_b, rx, d_img, img1, img1_b, rx1, d_img1,
    txt2_b, grad, d_proj, grad1, d_proj1,
):
    txt2_b[...] = unit(text2[...].astype(F32))[0].astype(B16)
    d_proj[...] = after(scale, bias, txt2_b, img, img_b, rx, d_img, grad)
    d_proj1[...] = after(scale, bias, txt2_b, img1, img1_b, rx1, d_img1, grad1)


def second_kernel(
    scale, bias, feat, whole, txt_b, txt2_b, feat0, d_proj0, feat1, d_proj1,
    img_b, grad0, grad2, part,
    img, rx, d_img, feats, d_proj,
):
    before_kernel(scale, bias, feat, whole, txt_b, img, img_b, rx, grad0, d_img)
    d_proj[ROWS + FEATS[0] :, :] = after(scale, bias, txt2_b, img, img_b, rx, d_img, grad2)
    for at, rows, grad in ((0, feat0, d_proj0), (ROWS, feat1, d_proj1)):
        feats[at : at + rows.shape[0], :] = rows[...]
        d_proj[at : at + rows.shape[0], :] = grad[...]
    feats[ROWS + FEATS[0] :, :] = feat[...]
    part[...] = dot32(feats[...], d_proj[...], FIRST)


def last_kernel(
    index, scale, bias, feat, whole, txt_b, txt2_b, part_in,
    img_b, grad0, grad2, keep, send,
    img, rx, d_img, part,
):
    before_kernel(scale, bias, feat, whole, txt_b, img, img_b, rx, grad0, d_img)
    d_proj = after(scale, bias, txt2_b, img, img_b, rx, d_img, grad2)
    part[...] = part_in[...] + dot32(feat[...], d_proj, FIRST)
    c = index[2]
    for zl in range(2):
        rows = pl.ds(zl * BLOCK, BLOCK)
        keep[rows, :] = part[pl.ds(pl.multiple_of((zl * 2 + c) * BLOCK, 8), BLOCK), :]
        gone = part[pl.ds(pl.multiple_of((zl * 2 + 1 - c) * BLOCK, 8), BLOCK), :]
        send[rows, :] = gone.astype(B16)


def text_sum(grads, imgs):
    total = dot32(grads[0][...], imgs[0][...], FIRST)
    for grad, img in zip(grads[1:], imgs[1:]):
        total = total + dot32(grad[...], img[...], FIRST)
    return total


def back_kernel(at, n, *refs):
    grads = [grad.at[:, at : at + n] for grad in refs[:4]]
    refs[8][...] = text_sum(grads, refs[4:8]).astype(B16)


def text_kernel(*refs):
    refs[8][...] = text_sum(refs[:4], refs[4:8])
    refs[9][0] = 0


def end_kernel(at, scale, text, d_txt_in, back, *refs):
    out, done, rows, sem = refs[-4:]
    n = rows.shape[0]
    txt, ry = unit(text[at : at + n, :].astype(F32))
    d_txt = scale[0] * (d_txt_in[at : at + n, :] + back[...].astype(F32))
    inner = jnp.sum(txt * d_txt, axis=-1, keepdims=True)
    rows[...] = ry * (d_txt - txt * inner)
    copy = pltpu.make_async_copy(rows, out.at[pl.ds(at, n)], sem)
    copy.start()
    copy.wait()
    done[0] = 0


def core_sum_kernel(index, keep, got, own, to1, to2, to3, total):
    total[...] = keep[...] + got[...].astype(F32)
    for d, ref in enumerate((own, to1, to2, to3)):
        z = (index[1] + d) % 4
        zl = z % 2
        at = pl.multiple_of(zl * BLOCK + z // 2 * HALF, 8)
        ref[...] = total[pl.ds(at, HALF), :].astype(ref.dtype)


def summed(own, *gots):
    value = own[...]
    for got in gots:
        value = value + got[...].astype(F32)
    return value


def z_sum_kernel(index, own, got1, got2, got3, done, mine, to1, to2, to3, total):
    x = index[0]
    total[HALF:, :] = jnp.zeros_like(total[HALF:, :])
    total[:HALF, :] = summed(own, got1, got2, got3)
    for d, ref in enumerate((mine, to1, to2, to3)):
        at = pl.multiple_of((x + d) % 4 * PART, 8)
        ref[...] = total[pl.ds(at, PART), :].astype(ref.dtype)


def x_sum_kernel(own, got1, got2, got3, came, held, total, send, passed):
    value = summed(own, got1, got2, got3)
    total[...] = value
    send[...] = value.astype(B16)


def y_sum_kernel(own, got1, got2, got3, send):
    send[...] = (summed(own, got1, got2, got3) / ROWS).astype(B16)


def pair_kernel(index, own, got, done, pair):
    zh = index[1] // 2
    pair[0] = jnp.where(zh == 0, own[...], got[...])
    pair[1] = jnp.where(zh == 0, got[...], own[...])


def gather_kernel(index, own, got1, got2, got3, after, out):
    for d, ref in enumerate((own, got1, got2, got3)):
        x = (index[0] + 4 - d) % 4
        for zh in range(2):
            value = ref[zh].astype(F32)
            at = pl.multiple_of(zh * HALF + x * PART, 8)

            @pl.when(x < 3)
            def _():
                out[pl.ds(at, PART), :] = value

            @pl.when(x == 3)
            def _():
                out[pl.ds(at, HALF - 3 * PART), :] = value[: HALF - 3 * PART, :]


def on_device(feat, text, head, partner, scale, bias):
    z = lax.axis_index("zh") * 2 + lax.axis_index("zl")
    index = jnp.stack([lax.axis_index("x"), z, lax.axis_index("c")]).astype(jnp.int32)
    half = BLOCK // 2

    n_a, n_b, n_c = FEATS
    top, bottom = cut([head], [(0, 0, half), (0, half, half)])
    text2 = along_dp(text, 2)
    up = moved(top, lambda x, y, z, c: (x, y, z - 1, c))
    down = moved(bottom, lambda x, y, z, c: (x, y, z + 1, c))
    far = to_core(head)
    full = (ROWS, WIDTH)
    square = (WIDTH, WIDTH)
    txt_b, near, who, feat_a, feat_b, feat_c, done = call(
        prepare_kernel,
        [(full, B16), ((2 * BLOCK, WIDTH), B16), ((ROWS, 1), jnp.int32)]
        + [((n, WIDTH), B16) for n in FEATS]
        + [((1,), jnp.int32)],
        [index, feat, text, head, far, partner.reshape(ROWS, 1)],
        limit=6,
        work=0,
    )
    up, down, feat_a, feat_b = gate([up, down, feat_a, feat_b], done)
    far_up, far_down = to_core(up), to_core(down)
    feat1a, feat1b = along_dp(feat_a, -1), along_dp(feat_b, -1)
    whole, img, img_b, rx, grad0, d_img = call(
        own_kernel,
        [(square, B16), (full, F32), (full, B16), ((ROWS, 1), F32)]
        + [((ROWS, ROWS), B16), (full, F32)],
        [index, scale, bias, feat, txt_b, near, up, down, far_up, far_down, who],
        work=0,
    )
    (feat_c,) = gate([feat_c], rx)
    feat1c = along_dp(feat_c, -1)
    first = (n_a, WIDTH)
    img1, img1_b, rx1, grad10, d_img1 = call(
        before_kernel,
        [(first, F32), (first, B16), ((n_a, 1), F32), ((n_a, ROWS), B16), (first, F32)],
        [scale, bias, feat1a, whole, txt_b],
    )
    txt2_b, grad2, d_proj, grad12, d_proj1 = call(
        visit_kernel,
        [(full, B16), ((ROWS, ROWS), B16), (full, B16), ((n_a, ROWS), B16), (first, B16)],
        [scale, bias, text2, img, img_b, rx, d_img, img1, img1_b, rx1, d_img1],
    )
    held = (ROWS + n_a + n_b, WIDTH)
    second = (n_b, WIDTH)
    img2_b, grad20, grad22, part = call(
        second_kernel,
        [(second, B16), ((n_b, ROWS), B16), ((n_b, ROWS), B16), (square, F32)],
        [scale, bias, feat1b, whole, txt_b, txt2_b, feat, d_proj, feat1a, d_proj1],
        scratch=[pltpu.VMEM(second, F32), pltpu.VMEM((n_b, 1), F32), pltpu.VMEM(second, F32)]
        + [pltpu.VMEM(held, B16), pltpu.VMEM(held, B16)],
        limit=18,
    )
    grads0, grads2, imgs = [grad0, grad10, grad20], [grad2, grad12, grad22], [img_b, img1_b, img2_b]
    last = (n_c, WIDTH)
    img_b, grad0, grad2, keep, send = call(
        last_kernel,
        [(last, B16), ((n_c, ROWS), B16), ((n_c, ROWS), B16)]
        + [((2 * BLOCK, WIDTH), F32), ((2 * BLOCK, WIDTH), B16)],
        [index, scale, bias, feat1c, whole, txt_b, txt2_b, part],
        scratch=[
            pltpu.VMEM(last, F32), pltpu.VMEM((n_c, 1), F32),
            pltpu.VMEM(last, F32), pltpu.VMEM(square, F32),
        ],
        limit=14,
    )
    grads0, grads2, imgs = grads0 + [grad0], grads2 + [grad2], imgs + [img_b]

    def back_rows(at, n):
        (rows,) = call(
            functools.partial(back_kernel, at, n), [((n, WIDTH), B16)], [*grads2, *imgs]
        )
        return rows

    got = to_core(send)
    d_txt, done = call(
        text_kernel, [(full, F32), ((1,), jnp.int32)], [*grads0, *imgs]
    )
    back_a = along_dp(back_rows(0, BACKS[0]), -2)
    half = (HALF, WIDTH)
    small = (PART, WIDTH)
    own, *sends = call(
        core_sum_kernel,
        [(half, F32)] + [(half, B16)] * 3,
        [index, keep, got],
        scratch=[pltpu.VMEM((2 * BLOCK, WIDTH), F32)],
    )
    gots = [moved(sends[d - 1], lambda x, y, z, c, d=d: (x, y, z + d, c)) for d in (2, 1, 3)]
    own, *sends = call(
        z_sum_kernel,
        [(small, F32)] + [(small, B16)] * 3,
        [index, own, *gots, done],
        scratch=[pltpu.VMEM((4 * PART, WIDTH), F32)],
    )
    gots = [moved(sends[d - 1], lambda x, y, z, c, d=d: (x + d, y, z, c)) for d in (1, 2, 3)]
    back_b = back_rows(*BACKS)
    own, send, back_b = call(
        x_sum_kernel,
        [(small, F32), (small, B16), (back_b.shape, B16)],
        [own, *gots, back_a, back_b],
        anywhere=(4, 5),
        kept={5: 2},
        work=0,
    )
    gots = [moved(send, lambda x, y, z, c, d=d: (x, y + d, z, c)) for d in (1, 2, 3)]
    back_b = along_dp(back_b, -2)
    (send,) = call(y_sum_kernel, [(small, B16)], [own, *gots], work=5 * 10**9)
    got = moved(send, lambda x, y, z, c: (x, y, z + 2, c))

    def end_rows(at, back, *before):
        return pl.pallas_call(
            functools.partial(end_kernel, at),
            out_shape=[
                jax.ShapeDtypeStruct(full, F32), jax.ShapeDtypeStruct((1,), jnp.int32)
            ],
            in_specs=[pl.BlockSpec(memory_space=pltpu.SMEM)]
            + [pl.BlockSpec(memory_space=pltpu.VMEM)] * 3
            + [pl.BlockSpec(memory_space=pl.ANY)] * len(before),
            out_specs=[
                pl.BlockSpec(memory_space=pl.ANY), pl.BlockSpec(memory_space=pltpu.SMEM)
            ],
            scratch_shapes=[pltpu.VMEM(back.shape, F32), pltpu.SemaphoreType.DMA],
            input_output_aliases={4: 0} if before else {},
            compiler_params=pltpu.CompilerParams(vmem_limit_bytes=12 * 1024 * 1024),
        )(scale, text, d_txt, back, *before)

    text_grad, done = end_rows(0, back_a)
    (pair,) = call(pair_kernel, [((2, *small), B16)], [index, send, got, done])
    gots = [moved(pair, lambda x, y, z, c, d=d: (x + d, y, z, c)) for d in (1, 2, 3)]
    text_grad, done = end_rows(BACKS[0], back_b, text_grad)
    (head_grad,) = call(
        gather_kernel,
        [((BLOCK, WIDTH), F32)],
        [index, pair, *gots, done],
        work=0,
    )
    return (head_grad, text_grad)


def solution(mesh):
    whole = Mesh(mesh.devices.reshape(SIZES), AXES)
    rows = P(AXES, None)
    fsdp = P(("zl", "c"), None)
    return jax.shard_map(
        on_device,
        mesh=whole,
        in_specs=(rows, rows, fsdp, P(AXES), P(), P()),
        out_specs=(fsdp, rows),
        check_vma=False,
    )
```

```python
import functools

import jax
import jax.numpy as jnp
from jax import lax
from jax.experimental import pallas as pl
from jax.experimental.pallas import tpu as pltpu
from jax.sharding import Mesh, PartitionSpec as P

AXES = ("x", "y", "zh", "zl", "c")
SIZES = (4, 4, 2, 2, 2)
ROWS = 768
WIDTH = 1152
BLOCK = 288
HALF = 144
PART = 40
FEATS = (256, 256, 256)
BACKS = (512, 256)
F32 = jnp.float32
B16 = jnp.bfloat16
PLAIN = (((1,), (0,)), ((), ()))
FIRST = (((0,), (0,)), ((), ()))
LAST = (((1,), (1,)), ((), ()))


def index_of(x, y, z, c):
    return ((x % 4 * 4 + y % 4) * 4 + z % 4) * 2 + c


def moved(value, target):
    pairs = [
        (index_of(x, y, z, c), index_of(*target(x, y, z, c)))
        for x in range(4)
        for y in range(4)
        for z in range(4)
        for c in range(2)
    ]
    return lax.ppermute(value, AXES, pairs)


def along_dp(value, by):
    pairs = [(d * 4 + j, (d + by) % 32 * 4 + j) for d in range(32) for j in range(4)]
    return lax.ppermute(value, AXES, pairs)


def to_core(value):
    return moved(value, lambda x, y, z, c: (x, y, z, 1 - c))


def call(kernel, outs, ins, scratch=(), aliases=None, limit=12, work=0, anywhere=(), kept=None, stays=()):
    specs = [pltpu.SMEM if a.size < 16 else pltpu.VMEM for a in ins]
    out_specs = [pltpu.SMEM if len(s) == 1 else pltpu.VMEM for s, t in outs]
    for k in anywhere:
        specs[k] = pl.ANY
    for k in (*(kept or {}).values(), *stays):
        out_specs[k] = pl.ANY
    return pl.pallas_call(
        kernel,
        out_shape=[jax.ShapeDtypeStruct(s, t) for s, t in outs],
        in_specs=[pl.BlockSpec(memory_space=s) for s in specs],
        out_specs=[pl.BlockSpec(memory_space=s) for s in out_specs],
        scratch_shapes=list(scratch),
        input_output_aliases={**(aliases or {}), **(kept or {})},
        cost_estimate=pl.CostEstimate(flops=work, bytes_accessed=0, transcendentals=0),
        compiler_params=pltpu.CompilerParams(vmem_limit_bytes=limit * 1024 * 1024),
    )(*ins)


def cut(arrays, pieces):
    def kernel(*refs):
        ins, outs, sems = refs[: len(arrays)], refs[len(arrays) : -1], refs[-1]
        copies = [
            pltpu.make_async_copy(ins[k].at[pl.ds(at, n)], out, sems.at[i])
            for i, ((k, at, n), out) in enumerate(zip(pieces, outs))
        ]
        for copy in copies:
            copy.start()
        for copy in copies:
            copy.wait()

    return pl.pallas_call(
        kernel,
        out_shape=[jax.ShapeDtypeStruct((n, WIDTH), B16) for _, _, n in pieces],
        in_specs=[pl.BlockSpec(memory_space=pl.ANY)] * len(arrays),
        out_specs=[pl.BlockSpec(memory_space=pl.ANY)] * len(pieces),
        scratch_shapes=[pltpu.SemaphoreType.DMA((len(pieces),))],
        cost_estimate=pl.CostEstimate(flops=0, bytes_accessed=0, transcendentals=0),
        compiler_params=pltpu.CompilerParams(vmem_limit_bytes=2 * 1024 * 1024),
    )(*arrays)


def gate(values, *after):
    n = len(values)
    return pl.pallas_call(
        lambda *refs: None,
        out_shape=[jax.ShapeDtypeStruct(v.shape, v.dtype) for v in values],
        in_specs=[
            pl.BlockSpec(memory_space=pltpu.SMEM if v.size == 1 else pl.ANY)
            for v in (*values, *after)
        ],
        out_specs=[pl.BlockSpec(memory_space=pl.ANY)] * n,
        input_output_aliases={k: k for k in range(n)},
        cost_estimate=pl.CostEstimate(flops=0, bytes_accessed=0, transcendentals=0),
        compiler_params=pltpu.CompilerParams(vmem_limit_bytes=2 * 1024 * 1024),
    )(*values, *after)


def dot32(a, b, dims=PLAIN):
    return lax.dot_general(a, b, dims, preferred_element_type=F32)


def unit(vec):
    inv = lax.rsqrt(jnp.sum(vec * vec, axis=-1, keepdims=True) + 1e-06)
    return (vec * inv, inv)


def probability(img_b, txt, scale_ref, bias_ref):
    return jax.nn.sigmoid(scale_ref[0] * dot32(img_b, txt, LAST) + bias_ref[0])


def project(feat_ref, whole_ref, img_ref, img_b_ref, rx_ref):
    img, rx = unit(dot32(feat_ref[...], whole_ref[...]))
    img_ref[...] = img
    img_b_ref[...] = img.astype(B16)
    rx_ref[...] = rx


def d_projection(img, rx, d_img, scale):
    d_img = scale[0] * d_img
    inner = jnp.sum(img * d_img, axis=-1, keepdims=True)
    return (rx * (d_img - img * inner)).astype(B16)


def prepare_kernel(
    index, feat, text, head, far, partner, txt_b, near, who, feat_a, feat_b, feat_c, done
):
    c = index[2]
    txt_b[...] = unit(text[...].astype(F32))[0].astype(B16)
    near[pl.ds(pl.multiple_of(c * BLOCK, 16), BLOCK), :] = head[...]
    near[pl.ds(pl.multiple_of((1 - c) * BLOCK, 16), BLOCK), :] = far[...]
    who[...] = partner[...]
    at = 0
    for piece in (feat_a, feat_b, feat_c):
        piece[...] = feat[at : at + piece.shape[0], :]
        at += piece.shape[0]
    done[0] = 0


def own_kernel(
    index, scale, bias, feat, txt_b, near, up, down, far_up, far_down, who,
    whole, img, img_b, rx, grad0, d_img,
):
    zl, c = index[1] % 2, index[2]
    away = (1 - zl) * 2

    def put(ref, at):
        whole[pl.ds(pl.multiple_of(at, 16), ref.shape[0]), :] = ref[...]

    put(near, zl * 2 * BLOCK)
    put(up, (away + c) * BLOCK)
    put(down, (away + c) * BLOCK + BLOCK // 2)
    put(far_up, (away + 1 - c) * BLOCK)
    put(far_down, (away + 1 - c) * BLOCK + BLOCK // 2)
    project(feat, whole, img, img_b, rx)
    label = lax.broadcasted_iota(jnp.int32, (ROWS, ROWS), 1) == who[...]
    grad = probability(img_b[...], txt_b[...], scale, bias) - label.astype(F32)
    grad0[...] = grad.astype(B16)
    d_img[...] = dot32(grad0[...], txt_b[...])


def before_kernel(scale, bias, feat, whole, txt_b, img, img_b, rx, grad0, d_img):
    project(feat, whole, img, img_b, rx)
    grad0[...] = probability(img_b[...], txt_b[...], scale, bias).astype(B16)
    d_img[...] = dot32(grad0[...], txt_b[...])


def after(scale, bias, txt2_b, img, img_b, rx, d_img, grad):
    grad[...] = probability(img_b[...], txt2_b[...], scale, bias).astype(B16)
    total = d_img[...] + dot32(grad[...], txt2_b[...])
    return d_projection(img[...], rx[...], total, scale)


def visit_kernel(
    scale, bias, text2, img, img_b, rx, d_img, img1, img1_b, rx1, d_img1,
    txt2_b, grad, d_proj, grad1, d_proj1,
):
    txt2_b[...] = unit(text2[...].astype(F32))[0].astype(B16)
    d_proj[...] = after(scale, bias, txt2_b, img, img_b, rx, d_img, grad)
    d_proj1[...] = after(scale, bias, txt2_b, img1, img1_b, rx1, d_img1, grad1)


def second_kernel(
    scale, bias, feat, whole, txt_b, txt2_b, feat0, d_proj0, feat1, d_proj1,
    img_b, grad0, grad2, part,
    img, rx, d_img, feats, d_proj,
):
    before_kernel(scale, bias, feat, whole, txt_b, img, img_b, rx, grad0, d_img)
    d_proj[ROWS + FEATS[0] :, :] = after(scale, bias, txt2_b, img, img_b, rx, d_img, grad2)
    for at, rows, grad in ((0, feat0, d_proj0), (ROWS, feat1, d_proj1)):
        feats[at : at + rows.shape[0], :] = rows[...]
        d_proj[at : at + rows.shape[0], :] = grad[...]
    feats[ROWS + FEATS[0] :, :] = feat[...]
    part[...] = dot32(feats[...], d_proj[...], FIRST)


def last_kernel(
    index, scale, bias, feat, whole, txt_b, txt2_b, part_in,
    img_b, grad0, grad2, keep, send,
    img, rx, d_img, part,
):
    before_kernel(scale, bias, feat, whole, txt_b, img, img_b, rx, grad0, d_img)
    d_proj = after(scale, bias, txt2_b, img, img_b, rx, d_img, grad2)
    part[...] = part_in[...] + dot32(feat[...], d_proj, FIRST)
    c = index[2]
    for zl in range(2):
        rows = pl.ds(zl * BLOCK, BLOCK)
        keep[rows, :] = part[pl.ds(pl.multiple_of((zl * 2 + c) * BLOCK, 8), BLOCK), :]
        gone = part[pl.ds(pl.multiple_of((zl * 2 + 1 - c) * BLOCK, 8), BLOCK), :]
        send[rows, :] = gone.astype(B16)


def text_sum(grads, imgs):
    total = dot32(grads[0][...], imgs[0][...], FIRST)
    for grad, img in zip(grads[1:], imgs[1:]):
        total = total + dot32(grad[...], img[...], FIRST)
    return total


def back_kernel(at, n, *refs):
    grads = [grad.at[:, at : at + n] for grad in refs[:4]]
    refs[8][...] = text_sum(grads, refs[4:8]).astype(B16)


def text_kernel(*refs):
    refs[8][...] = text_sum(refs[:4], refs[4:8])
    refs[9][0] = 0


def end_kernel(at, scale, text, d_txt_in, back, *refs):
    out, done, rows, sem = refs[-4:]
    n = rows.shape[0]
    txt, ry = unit(text[at : at + n, :].astype(F32))
    d_txt = scale[0] * (d_txt_in[at : at + n, :] + back[...].astype(F32))
    inner = jnp.sum(txt * d_txt, axis=-1, keepdims=True)
    rows[...] = ry * (d_txt - txt * inner)
    copy = pltpu.make_async_copy(rows, out.at[pl.ds(at, n)], sem)
    copy.start()
    copy.wait()
    done[0] = 0


def core_sum_kernel(index, keep, got, own, to1, to2, to3, total):
    total[...] = keep[...] + got[...].astype(F32)
    for d, ref in enumerate((own, to1, to2, to3)):
        z = (index[1] + d) % 4
        zl = z % 2
        at = pl.multiple_of(zl * BLOCK + z // 2 * HALF, 8)
        ref[...] = total[pl.ds(at, HALF), :].astype(ref.dtype)


def summed(own, *gots):
    value = own[...]
    for got in gots:
        value = value + got[...].astype(F32)
    return value


def z_sum_kernel(index, own, got1, got2, got3, done, mine, to1, to2, to3, total):
    x = index[0]
    total[HALF:, :] = jnp.zeros_like(total[HALF:, :])
    total[:HALF, :] = summed(own, got1, got2, got3)
    for d, ref in enumerate((mine, to1, to2, to3)):
        at = pl.multiple_of((x + d) % 4 * PART, 8)
        ref[...] = total[pl.ds(at, PART), :].astype(ref.dtype)


def x_sum_kernel(own, got1, got2, got3, came, held, total, send, passed):
    value = summed(own, got1, got2, got3)
    total[...] = value
    send[...] = value.astype(B16)


def y_sum_kernel(own, got1, got2, got3, send):
    send[...] = (summed(own, got1, got2, got3) / ROWS).astype(B16)


def pair_kernel(index, own, got, done, pair):
    zh = index[1] // 2
    pair[0] = jnp.where(zh == 0, own[...], got[...])
    pair[1] = jnp.where(zh == 0, got[...], own[...])


def gather_kernel(index, own, got1, got2, got3, after, out, rows, sems):
    short = HALF - 3 * PART
    for d, ref in enumerate((own, got1, got2, got3)):
        x = (index[0] + 4 - d) % 4
        for zh in range(2):
            k = d * 2 + zh
            rows[k] = ref[zh].astype(F32)
            at = pl.multiple_of(zh * HALF + x * PART, 8)

            @pl.when(x < 3)
            def _():
                pltpu.make_async_copy(rows.at[k], out.at[pl.ds(at, PART)], sems.at[k]).start()

            @pl.when(x == 3)
            def _():
                pltpu.make_async_copy(
                    rows.at[k, pl.ds(0, short)], out.at[pl.ds(at, short)], sems.at[k]
                ).start()

    for d in range(4):
        x = (index[0] + 4 - d) % 4
        for zh in range(2):
            k = d * 2 + zh

            @pl.when(x < 3)
            def _():
                pltpu.make_async_copy(rows.at[k], out.at[pl.ds(0, PART)], sems.at[k]).wait()

            @pl.when(x == 3)
            def _():
                pltpu.make_async_copy(
                    rows.at[k, pl.ds(0, short)], out.at[pl.ds(0, short)], sems.at[k]
                ).wait()


def on_device(feat, text, head, partner, scale, bias):
    z = lax.axis_index("zh") * 2 + lax.axis_index("zl")
    index = jnp.stack([lax.axis_index("x"), z, lax.axis_index("c")]).astype(jnp.int32)
    half = BLOCK // 2

    n_a, n_b, n_c = FEATS
    top, bottom = cut([head], [(0, 0, half), (0, half, half)])
    text2 = along_dp(text, 2)
    up = moved(top, lambda x, y, z, c: (x, y, z - 1, c))
    down = moved(bottom, lambda x, y, z, c: (x, y, z + 1, c))
    far = to_core(head)
    full = (ROWS, WIDTH)
    square = (WIDTH, WIDTH)
    txt_b, near, who, feat_a, feat_b, feat_c, done = call(
        prepare_kernel,
        [(full, B16), ((2 * BLOCK, WIDTH), B16), ((ROWS, 1), jnp.int32)]
        + [((n, WIDTH), B16) for n in FEATS]
        + [((1,), jnp.int32)],
        [index, feat, text, head, far, partner.reshape(ROWS, 1)],
        limit=6,
        work=0,
    )
    up, down, feat_a, feat_b = gate([up, down, feat_a, feat_b], done)
    far_up, far_down = to_core(up), to_core(down)
    feat1a, feat1b = along_dp(feat_a, -1), along_dp(feat_b, -1)
    whole, img, img_b, rx, grad0, d_img = call(
        own_kernel,
        [(square, B16), (full, F32), (full, B16), ((ROWS, 1), F32)]
        + [((ROWS, ROWS), B16), (full, F32)],
        [index, scale, bias, feat, txt_b, near, up, down, far_up, far_down, who],
        work=0,
    )
    (feat_c,) = gate([feat_c], rx)
    feat1c = along_dp(feat_c, -1)
    first = (n_a, WIDTH)
    img1, img1_b, rx1, grad10, d_img1 = call(
        before_kernel,
        [(first, F32), (first, B16), ((n_a, 1), F32), ((n_a, ROWS), B16), (first, F32)],
        [scale, bias, feat1a, whole, txt_b],
    )
    txt2_b, grad2, d_proj, grad12, d_proj1 = call(
        visit_kernel,
        [(full, B16), ((ROWS, ROWS), B16), (full, B16), ((n_a, ROWS), B16), (first, B16)],
        [scale, bias, text2, img, img_b, rx, d_img, img1, img1_b, rx1, d_img1],
    )
    held = (ROWS + n_a + n_b, WIDTH)
    second = (n_b, WIDTH)
    img2_b, grad20, grad22, part = call(
        second_kernel,
        [(second, B16), ((n_b, ROWS), B16), ((n_b, ROWS), B16), (square, F32)],
        [scale, bias, feat1b, whole, txt_b, txt2_b, feat, d_proj, feat1a, d_proj1],
        scratch=[pltpu.VMEM(second, F32), pltpu.VMEM((n_b, 1), F32), pltpu.VMEM(second, F32)]
        + [pltpu.VMEM(held, B16), pltpu.VMEM(held, B16)],
        limit=18,
    )
    grads0, grads2, imgs = [grad0, grad10, grad20], [grad2, grad12, grad22], [img_b, img1_b, img2_b]
    last = (n_c, WIDTH)
    img_b, grad0, grad2, keep, send = call(
        last_kernel,
        [(last, B16), ((n_c, ROWS), B16), ((n_c, ROWS), B16)]
        + [((2 * BLOCK, WIDTH), F32), ((2 * BLOCK, WIDTH), B16)],
        [index, scale, bias, feat1c, whole, txt_b, txt2_b, part],
        scratch=[
            pltpu.VMEM(last, F32), pltpu.VMEM((n_c, 1), F32),
            pltpu.VMEM(last, F32), pltpu.VMEM(square, F32),
        ],
        limit=14,
    )
    grads0, grads2, imgs = grads0 + [grad0], grads2 + [grad2], imgs + [img_b]

    def back_rows(at, n):
        (rows,) = call(
            functools.partial(back_kernel, at, n), [((n, WIDTH), B16)], [*grads2, *imgs]
        )
        return rows

    got = to_core(send)
    d_txt, done = call(
        text_kernel, [(full, F32), ((1,), jnp.int32)], [*grads0, *imgs]
    )
    back_a = along_dp(back_rows(0, BACKS[0]), -2)
    half = (HALF, WIDTH)
    small = (PART, WIDTH)
    own, *sends = call(
        core_sum_kernel,
        [(half, F32)] + [(half, B16)] * 3,
        [index, keep, got],
        scratch=[pltpu.VMEM((2 * BLOCK, WIDTH), F32)],
    )
    gots = [moved(sends[d - 1], lambda x, y, z, c, d=d: (x, y, z + d, c)) for d in (2, 1, 3)]
    own, *sends = call(
        z_sum_kernel,
        [(small, F32)] + [(small, B16)] * 3,
        [index, own, *gots, done],
        scratch=[pltpu.VMEM((4 * PART, WIDTH), F32)],
    )
    gots = [moved(sends[d - 1], lambda x, y, z, c, d=d: (x + d, y, z, c)) for d in (1, 2, 3)]
    back_b = back_rows(*BACKS)
    own, send, back_b = call(
        x_sum_kernel,
        [(small, F32), (small, B16), (back_b.shape, B16)],
        [own, *gots, back_a, back_b],
        anywhere=(4, 5),
        kept={5: 2},
        work=0,
    )
    gots = [moved(send, lambda x, y, z, c, d=d: (x, y + d, z, c)) for d in (1, 2, 3)]
    back_b = along_dp(back_b, -2)
    (send,) = call(y_sum_kernel, [(small, B16)], [own, *gots], work=5 * 10**9)
    got = moved(send, lambda x, y, z, c: (x, y, z + 2, c))

    def end_rows(at, back, *before):
        return pl.pallas_call(
            functools.partial(end_kernel, at),
            out_shape=[
                jax.ShapeDtypeStruct(full, F32), jax.ShapeDtypeStruct((1,), jnp.int32)
            ],
            in_specs=[pl.BlockSpec(memory_space=pltpu.SMEM)]
            + [pl.BlockSpec(memory_space=pltpu.VMEM)] * 3
            + [pl.BlockSpec(memory_space=pl.ANY)] * len(before),
            out_specs=[
                pl.BlockSpec(memory_space=pl.ANY), pl.BlockSpec(memory_space=pltpu.SMEM)
            ],
            scratch_shapes=[pltpu.VMEM(back.shape, F32), pltpu.SemaphoreType.DMA],
            input_output_aliases={4: 0} if before else {},
            compiler_params=pltpu.CompilerParams(vmem_limit_bytes=12 * 1024 * 1024),
        )(scale, text, d_txt, back, *before)

    text_grad, done = end_rows(0, back_a)
    (pair,) = call(pair_kernel, [((2, *small), B16)], [index, send, got, done])
    gots = [moved(pair, lambda x, y, z, c, d=d: (x + d, y, z, c)) for d in (1, 2, 3)]
    text_grad, done = end_rows(BACKS[0], back_b, text_grad)
    (head_grad,) = call(
        gather_kernel,
        [((BLOCK, WIDTH), F32)],
        [index, pair, *gots, done],
        scratch=[pltpu.VMEM((8, PART, WIDTH), F32), pltpu.SemaphoreType.DMA((8,))],
        stays=(0,),
        work=0,
    )
    return (head_grad, text_grad)


def solution(mesh):
    whole = Mesh(mesh.devices.reshape(SIZES), AXES)
    rows = P(AXES, None)
    fsdp = P(("zl", "c"), None)
    return jax.shard_map(
        on_device,
        mesh=whole,
        in_specs=(rows, rows, fsdp, P(AXES), P(), P()),
        out_specs=(fsdp, rows),
        check_vma=False,
    )
```
